128 devices in a mesh: row: 8 (over z_lo, y), col: 16 (over x, z_hi, core).
Axes of the slice: x: 4, y: 4, z: 4 (z_hi: 2, z_lo: 2; z = z_hi * 2 + z_lo), core: 2. Of those that a mesh axis runs over, the one named last changes fastest.
Arguments:
- children: float32 [24576, 12288], P('row', 'col'), as said below
- parent: float32 [16384, 16384], P('row', 'col'), as said below
- relay_map: int32 [2, 46], replicated, may hold values from 0 to 63, as said below
Outputs:
- parent_out: float32 [16384, 16384], P('row', 'col')
- child_factor: float32 [24576, 512], P('row', 'col')
The draws below stay inside these ranges and needn't reach their ends.
Inputs may be any that keep to these rules, and one draw needn't show every extreme that they name: children holds two symmetric positive definite fronts. parent is symmetric positive definite. relay_map[k, j - 2] is the parent block that receives child k's block j (blocks of 256); it lies in [8 * (j // 6), 8 * (j // 6) + 8); entries of one child are distinct.
All inputs are finite; a program needn't handle non-finite values.
Results may differ from the reference program's by a relative error of at most 0.0001.
Values sent between devices are 32-bit elements; how exact they have to be, the bound alone decides.
A program may use at most 192 MiB of HBM per device.

```python
import math
import jax
import jax.numpy as jnp
from jax import lax

FC = 12288
FP = 16384
NB = 256
PIV_C = 512
PIV_P = 512
RC = 3072
GC = 6
GP = 8
N_ROW = 8


def symmetric_fronts(base_values, diagonal, coupling, matrix_order):
    mixed = (base_values + jnp.swapaxes(base_values, -1, -2)) * (1.6 / math.sqrt(matrix_order))
    mixed = mixed + coupling[..., :, None] * coupling[..., None, :]
    return mixed + diagonal[..., :, None] * jnp.eye(matrix_order, dtype=jnp.float32)


def draw_children(key, part):
    key = jax.random.fold_in(key, 11)
    key_base, key_diag, key_couple = jax.random.split(key, 3)
    base_values = jax.random.truncated_normal(key_base, -4.0, 4.0, (2, FC, FC), jnp.float32)
    diagonal = jax.random.uniform(key_diag, (2, FC), jnp.float32, 4.4, 6.4)
    coupling = jax.random.uniform(key_couple, (2, FC), jnp.float32, 0.15, 0.3)
    fronts = symmetric_fronts(base_values, diagonal, coupling, FC)
    half_rows = N_ROW // 2
    return fronts.reshape(2, half_rows, RC, FC).transpose(1, 0, 2, 3).reshape(2 * FC, FC)


def draw_parent(key, part):
    key = jax.random.fold_in(key, 12)
    key_base, key_diag, key_couple = jax.random.split(key, 3)
    base_values = jax.random.truncated_normal(key_base, -4.0, 4.0, (FP, FP), jnp.float32)
    diagonal = jax.random.uniform(key_diag, (FP,), jnp.float32, 4.4, 6.4)
    coupling = jax.random.uniform(key_couple, (FP,), jnp.float32, 0.15, 0.3)
    return symmetric_fronts(base_values, diagonal, coupling, FP)


def draw_relay_map(key, part):
    key = jax.random.fold_in(key, 13)
    group_count = FC // NB // GC
    scores = jax.random.randint(key, (2, group_count, GP), 0, 1 << 20)
    scores = scores * GP + jnp.arange(GP, dtype=jnp.int32)[None, None, :]
    groups = jnp.arange(group_count, dtype=jnp.int32)[None, :, None]
    slots = jnp.arange(GP, dtype=jnp.int32)[None, None, :]
    first_forced = (groups == 0) & (slots == 0)
    last_forced = (groups == group_count - 1) & (slots == GP - 1)
    scores = jnp.where(first_forced | last_forced, -1, scores)
    chosen = jnp.argsort(scores, axis=-1)[:, :, :GC].astype(jnp.int32)
    chosen = jnp.roll(chosen, PIV_C // NB % GC, axis=-1)
    offsets = (jnp.arange(group_count, dtype=jnp.int32) * GP)[None, :, None]
    mapped = (chosen + offsets).reshape(2, group_count * GC)
    return mapped[:, PIV_C // NB:].astype(jnp.int32)


def setup_inputs(seed: int = 0) -> dict:
    arg_keys = jax.random.split(jax.random.key(seed), 4)
    children = draw_children(jax.random.fold_in(arg_keys[3], 71), 0)
    parent = draw_parent(jax.random.fold_in(arg_keys[3], 71), 0)
    relay_map = draw_relay_map(jax.random.fold_in(arg_keys[3], 71), 0)
    return {"children": children, "parent": parent, "relay_map": relay_map}


def lower_solve(diag_factor, right_side):
    return lax.linalg.triangular_solve(diag_factor, right_side, left_side=True, lower=True)

def partial_cholesky(matrix, pivots):
    matrix_order = matrix.shape[0]
    factor = jnp.zeros((matrix_order, pivots), jnp.float32)
    for panel_index in range(pivots // NB):
        low_edge = panel_index * NB
        high_edge = low_edge + NB
        diag_factor = jnp.linalg.cholesky(matrix[low_edge:high_edge, low_edge:high_edge])
        beneath = lower_solve(diag_factor, matrix[high_edge:, low_edge:high_edge].T).T
        update = jnp.dot(beneath, beneath.T, precision=lax.Precision.HIGHEST)
        matrix = matrix.at[high_edge:, high_edge:].add(-update)
        factor = factor.at[low_edge:high_edge, low_edge:high_edge].set(diag_factor)
        factor = factor.at[high_edge:, low_edge:high_edge].set(beneath)
    return (matrix, factor)

def reference(children, parent, relay_map):
    half_rows = N_ROW // 2
    rows_each = FC // half_rows
    stacked = children.reshape(half_rows, 2, rows_each, FC)
    parent_blocks = FP // NB
    tail_blocks = (FC - PIV_C) // NB
    assembled = parent.reshape(parent_blocks, NB, parent_blocks, NB).transpose(0, 2, 1, 3)
    factors = []
    for member in range(2):
        child = stacked[:, member].reshape(FC, FC)
        reduced, factor = partial_cholesky(child, PIV_C)
        factors.append(factor)
        blocks_view = reduced[PIV_C:, PIV_C:].reshape(tail_blocks, NB, tail_blocks, NB).transpose(0, 2, 1, 3)
        targets = relay_map[member]
        assembled = assembled.at[targets[:, None], targets[None, :]].add(blocks_view)
    combined = assembled.transpose(0, 2, 1, 3).reshape(FP, FP)
    reduced_parent, parent_factor = partial_cholesky(combined, PIV_P)
    parent_out = reduced_parent.at[:, :PIV_P].set(parent_factor).at[:PIV_P, PIV_P:].set(0.0)
    child_factor = jnp.stack(factors).reshape(2, half_rows, rows_each, PIV_C).transpose(1, 0, 2, 3).reshape(2 * FC, PIV_C)
    return (parent_out, child_factor)
```

```python
import functools

import jax
import jax.numpy as jnp
from jax import lax
from jax.experimental import pallas as pl
from jax.experimental.pallas import tpu as pltpu
from jax.sharding import PartitionSpec as P

NB = 256
PIV = 512
HI = lax.Precision.HIGHEST
MESH = pl.DeviceIdType.MESH
F32 = jnp.float32

def nt(a, b):
    return lax.dot_general(a, b, (((1,), (1,)), ((), ())), precision=HI, preferred_element_type=jnp.float32)

def nn(a, b):
    return lax.dot_general(a, b, (((1,), (0,)), ((), ())), precision=HI, preferred_element_type=jnp.float32)

def diag_inverse(work, s):
    tiles = [work[pl.ds(s + 8 * t, 8), pl.ds(s, 128)] for t in range(16)]
    rows8 = lax.broadcasted_iota(jnp.int32, (8, 128), 0)
    lanes = lax.broadcasted_iota(jnp.int32, (8, 128), 1)
    unit = [jnp.where(rows8 + 8 * t == lanes, 1.0, 0.0) for t in range(16)]
    scales = [jnp.zeros((8, 1), jnp.float32) for t in range(16)]
    for j in range(128):
        tj, i = j // 8, j % 8
        pivot = tiles[tj][i:i + 1, j:j + 1]
        inv = 1.0 / pivot
        row = tiles[tj][i:i + 1, :] * inv
        mrow = unit[tj][i:i + 1, :] * inv
        for t in range(tj, 16):
            col = tiles[t][:, j:j + 1]
            if t == tj:
                col = jnp.where(rows8[:, :1] > i, col, 0.0)
            tiles[t] = tiles[t] - col * row
            unit[t] = unit[t] - col * mrow
    out = []
    for t in range(16):
        d = jnp.sum(jnp.where(rows8 + 8 * t == lanes, tiles[t], 0.0), axis=1, keepdims=True)
        out.append(unit[t] * lax.rsqrt(d))
    return jnp.concatenate(out, axis=0)

def factor_inverse(work, low, inv, di):
    n = 512
    inv[...] = jnp.zeros_like(inv)
    low[...] = jnp.zeros_like(low)
    def step(b, _):
        s = pl.multiple_of(b * 128, 128)
        d = diag_inverse(work, s)
        panel = work[:, pl.ds(s, 128)]
        l21 = nt(panel, d)
        ids = lax.broadcasted_iota(jnp.int32, (n, 128), 0)
        l21 = jnp.where(ids >= s + 128, l21, 0.0)
        left = nn(low[pl.ds(s, 128), :], inv[...])
        inv[pl.ds(s, 128), :] = -nn(d, left)
        inv[pl.ds(s, 128), pl.ds(s, 128)] = d
        low[:, pl.ds(s, 128)] = l21
        work[...] = work[...] - nt(l21, l21)
        return 0
    lax.fori_loop(0, 4, step, 0)

def factor_kernel(a_ref, inv_ref, work, low):
    work[...] = a_ref[...]
    factor_inverse(work, low, inv_ref, None)


def leading_inverse(matrix):
    return pl.pallas_call(
        factor_kernel,
        grid=(1,),
        out_shape=jax.ShapeDtypeStruct((PIV, PIV), F32),
        in_specs=[pl.BlockSpec((PIV, PIV), lambda i: (0, 0))],
        out_specs=pl.BlockSpec((PIV, PIV), lambda i: (0, 0)),
        scratch_shapes=[pltpu.VMEM((PIV, PIV), F32)] * 2,
        compiler_params=pltpu.CompilerParams(vmem_limit_bytes=32 << 20),
        cost_estimate=pl.CostEstimate(flops=10**10, bytes_accessed=1 << 21, transcendentals=0),
        name="leading_inverse",
    )(matrix)


def send(src, dst, send_sem, recv_sem, **device):
    return pltpu.make_async_remote_copy(
        src_ref=src,
        dst_ref=dst,
        send_sem=send_sem,
        recv_sem=recv_sem,
        device_id=device,
        device_id_type=MESH,
    )


def panels_kernel(
    members,
    src,
    inverse,
    rows,
    cols,
    inv,
    row_put,
    row_got,
    row_out,
    row_in,
    row_over,
    col_put,
    col_got,
    col_out,
    col_in,
    col_over,
    inv_put,
    inv_got,
    inv_down,
    inv_down_got,
    inv_out,
    inv_in,
    inv_over,
    here,
):
    r = lax.axis_index("row")
    c = lax.axis_index("col")
    g, h = c // 2, c % 2
    parity = r % 2
    other = c + 1 - 2 * h
    mate = r + 1 - 2 * parity
    piece = rows.shape[3]
    strip = cols.shape[2] // 8
    own = parity if members == 2 else 0

    barrier = pltpu.get_barrier_semaphore()
    count = 0
    for d in range(1, 8):
        pl.semaphore_signal(barrier, 1, device_id={"row": (r + d) % 8}, device_id_type=MESH)
        count += 1
    for d in range(1, 16):
        pl.semaphore_signal(barrier, 1, device_id={"col": (c + d) % 16}, device_id_type=MESH)
        count += 1
        if members == 2:
            pl.semaphore_signal(
                barrier, 1, device_id={"row": mate, "col": (c + d) % 16}, device_id_type=MESH
            )
            count += 1
    pl.semaphore_wait(barrier, count)

    def row_piece(target_row, dest):
        start = (dest % 2 * 8 + dest // 2) * piece
        if members == 2:
            start = start + target_row % 2 * (16 * piece)
        return src.at[pl.ds(pl.multiple_of(start, 8), piece), pl.ds(0, PIV)]

    def col_strip(dest):
        return src.at[pl.ds(pl.multiple_of(dest * strip, 8), strip), :]

    def col_slot(half, k, dest):
        return cols.at[half, k, pl.ds(pl.multiple_of(dest * strip, 8), strip), :]

    def row_scatter(d, own_row):
        dest = (c + d) % 16
        target = r if own_row else mate
        return send(
            row_piece(target, dest),
            rows.at[own, dest % 2, dest // 2],
            row_put.at[0 if own_row else 1, d],
            row_got.at[own],
            row=target,
            col=dest,
        )

    def col_scatter(k, d):
        dest = (r + d) % 8
        return send(
            col_strip(dest), col_slot(h, k, dest), col_put.at[d], col_got.at[k], row=dest, col=c
        )

    def inv_scatter(k, d):
        dest = (c + d) % 16
        at = (dest % 2 * 8 + dest // 2) * 32
        return send(
            inverse.at[pl.ds(pl.multiple_of(at, 8), 32), :],
            inv.at[k, dest % 2, dest // 2],
            inv_put.at[d],
            inv_got.at[k],
            row=r,
            col=dest,
        )

    local_row = pltpu.make_async_copy(row_piece(r, c), rows.at[own, h, g], here.at[0])
    local_col = pltpu.make_async_copy(col_strip(r), col_slot(h, r, r), here.at[1])
    local_inv = pltpu.make_async_copy(inverse.at[pl.ds(0, 32), :], inv.at[r, 0, 0], here.at[2])

    @pl.when(r < members)
    def _():
        local_col.start()

        @pl.loop(1, 8)
        def _(d):
            col_scatter(r, d).start()

    @pl.when(c == 0)
    def _():
        local_row.start()

        @pl.loop(1, 16)
        def _(d):
            row_scatter(d, True).start()

        if members == 2:
            row_scatter(0, False).start()

            @pl.loop(1, 16)
            def _(d):
                row_scatter(d, False).start()

    @pl.when((r < members) & (c == 0))
    def _():
        local_inv.start()

        @pl.loop(1, 16)
        def _(d):
            inv_scatter(r, d).start()

    def col_gather(k, d):
        return send(
            col_slot(h, k, r),
            col_slot(h, k, r),
            col_out.at[k, d],
            col_in.at[k, r],
            row=(r + d) % 8,
            col=c,
        )

    def col_arrival(k, d):
        sender = (r + d) % 8
        return send(
            col_slot(h, k, sender),
            col_slot(h, k, sender),
            col_out.at[k, d],
            col_in.at[k, sender],
            row=sender,
            col=c,
        )

    def row_gather(k, d):
        return send(
            rows.at[k, h, g],
            rows.at[k, h, g],
            row_out.at[k, d],
            row_in.at[k, g],
            row=r,
            col=(g + d) % 8 * 2 + h,
        )

    def row_arrival(k, d):
        sender = (g + d) % 8
        return send(
            rows.at[k, h, sender],
            rows.at[k, h, sender],
            row_out.at[k, d],
            row_in.at[k, sender],
            row=r,
            col=sender * 2 + h,
        )

    def inv_column(k, d):
        return send(
            inv.at[k, h, g],
            inv.at[k, h, g],
            inv_down.at[d],
            inv_down_got.at[k],
            row=(r + d) % 8,
            col=c,
        )

    def inv_gather(k, d):
        return send(
            inv.at[k, h, g],
            inv.at[k, h, g],
            inv_out.at[k, d],
            inv_in.at[k, g],
            row=r,
            col=(g + d) % 8 * 2 + h,
        )

    def inv_arrival(k, d):
        sender = (g + d) % 8
        return send(
            inv.at[k, h, sender],
            inv.at[k, h, sender],
            inv_out.at[k, d],
            inv_in.at[k, sender],
            row=r,
            col=sender * 2 + h,
        )

    for k in range(members):

        @pl.when(r == k)
        def _():
            local_col.wait()

        @pl.when(r != k)
        def _():
            col_scatter(k, 1).wait_recv()

        @pl.loop(1, 8)
        def _(d):
            col_gather(k, d).start()

    for k in range(members):
        mine = (c == 0) & (own == k)

        @pl.when(mine)
        def _():
            local_row.wait()

        @pl.when(jnp.logical_not(mine))
        def _():
            send(
                rows.at[k, h, g], rows.at[k, h, g], row_put.at[0, 0], row_got.at[k], row=r, col=other
            ).wait_recv()

        @pl.loop(1, 8)
        def _(d):
            row_gather(k, d).start()

    for k in range(members):

        @pl.when((r == k) & (c == 0))
        def _():
            local_inv.wait()

        @pl.when((r == k) & (c != 0))
        def _():
            inv_scatter(k, 1).wait_recv()

        @pl.when(r == k)
        def _():
            @pl.loop(1, 8)
            def _(d):
                inv_column(k, d).start()

    for k in range(members):

        @pl.when(r != k)
        def _():
            inv_column(k, 1).wait_recv()

        @pl.loop(1, 8)
        def _(d):
            inv_gather(k, d).start()

    def cross(buffer, half, sems):
        return send(buffer, buffer, sems.at[0], sems.at[1], row=r, col=other)

    def col_cross(half):
        return cross(cols.at[half], half, col_over)

    for k in range(members):

        @pl.loop(1, 8)
        def _(d):
            col_arrival(k, d).wait_recv()

    if members == 2:
        col_cross(h).start()
    for k in range(members):

        @pl.loop(1, 8)
        def _(d):
            row_arrival(k, d).wait_recv()

        cross(rows.at[k, h], h, row_over.at[k]).start()
    for k in range(members):

        @pl.loop(1, 8)
        def _(d):
            inv_arrival(k, d).wait_recv()

        cross(inv.at[k, h], h, inv_over.at[k]).start()

    if members == 2:
        col_cross(1 - h).wait_recv()
        col_cross(h).wait_send()
    for k in range(members):
        cross(rows.at[k, 1 - h], h, row_over.at[k]).wait_recv()
        cross(rows.at[k, h], h, row_over.at[k]).wait_send()
        cross(inv.at[k, 1 - h], h, inv_over.at[k]).wait_recv()
        cross(inv.at[k, h], h, inv_over.at[k]).wait_send()

        @pl.loop(1, 8)
        def _(d):
            col_gather(k, d).wait_send()
            row_gather(k, d).wait_send()
            inv_gather(k, d).wait_send()

        @pl.when(r == k)
        def _():
            @pl.loop(1, 8)
            def _(d):
                col_scatter(k, d).wait_send()
                inv_column(k, d).wait_send()

        @pl.when((r == k) & (c == 0))
        def _():
            @pl.loop(1, 16)
            def _(d):
                inv_scatter(k, d).wait_send()

    @pl.when(c == 0)
    def _():
        @pl.loop(1, 16)
        def _(d):
            row_scatter(d, True).wait_send()

        if members == 2:

            @pl.loop(0, 16)
            def _(d):
                row_scatter(d, False).wait_send()


def share_panels(members, source, inverse, piece, collective_id):
    width = source.shape[1]
    dma = pltpu.SemaphoreType.DMA
    out_shape = (
        jax.ShapeDtypeStruct((members, 2, 8, piece, PIV), F32),
        jax.ShapeDtypeStruct((2, members, PIV, width), F32),
        jax.ShapeDtypeStruct((members, 2, 8, 32, PIV), F32),
    )
    scratch = [
        dma((2, 16)),
        dma((members,)),
        dma((members, 8)),
        dma((members, 8)),
        dma((members, 2)),
        dma((8,)),
        dma((members,)),
        dma((members, 8)),
        dma((members, 8)),
        dma((2,)),
        dma((16,)),
        dma((members,)),
        dma((8,)),
        dma((members,)),
        dma((members, 8)),
        dma((members, 8)),
        dma((members, 2)),
        dma((3,)),
    ]
    rows, cols, inv = pl.pallas_call(
        functools.partial(panels_kernel, members),
        out_shape=out_shape,
        in_specs=[pl.BlockSpec(memory_space=pl.ANY)] * 2,
        out_specs=[pl.BlockSpec(memory_space=pl.ANY)] * 3,
        scratch_shapes=scratch,
        compiler_params=pltpu.CompilerParams(collective_id=collective_id, has_side_effects=True),
        cost_estimate=pl.CostEstimate(flops=10**10, bytes_accessed=1 << 25, transcendentals=0),
        name="share_panels_%d" % members,
    )(source, inverse)
    return (
        rows.reshape(members, 16 * piece, PIV),
        cols,
        inv.reshape(members, PIV, PIV),
    )


def split(value):
    high = value.astype(jnp.bfloat16)
    return high, (value - high.astype(F32)).astype(jnp.bfloat16)


def dot3(left, right):
    (lh, ll), (rh, rl) = left, right

    def one(a, b):
        return jnp.dot(a, b, preferred_element_type=F32)

    return one(lh, rh) + (one(lh, rl) + one(ll, rh))


def assemble_kernel(
    info,
    rowi,
    rowv,
    colj,
    colv,
    parent,
    rows0,
    rows1,
    cols,
    inv,
    *rest,
):
    blocks = rest[:16]
    out, high, low = rest[16:]
    t = pl.program_id(0)
    half = info[1]

    @pl.when(t == 0)
    def _():
        for m in range(2):
            k = info[0] if m == 0 else 1 - info[0]
            for u in range(4):
                j = colj[m, u]
                at = pl.multiple_of(j % 3 * NB, NB)
                block = cols[j // 3, k, :, pl.ds(at, NB)]
                solved = nn(inv[k], block)
                solved = jnp.where(colv[m, u] > 0, solved, 0.0)
                sh, sl = split(solved)
                high[m, :, u * NB : (u + 1) * NB] = sh
                low[m, :, u * NB : (u + 1) * NB] = sl

    total = parent[...]
    for m in range(2):
        k = info[0] if m == 0 else 1 - info[0]
        panel = (rows0, rows1)[m]
        solved = nt(panel[0], inv[k])
        solved = jnp.where(rowv[m, t] > 0, solved, 0.0)
        total = total - dot3(split(solved), (high[m], low[m]))
        adds = []
        for u in range(4):
            mine, theirs = blocks[m * 8 + u], blocks[m * 8 + 4 + u]
            use = (rowv[m, t] > 0) & (colv[m, u] > 0)
            block = jnp.where(colj[m, u] // 3 == half, mine[...], theirs[...])
            adds.append(jnp.where(use, block, 0.0))
        total = total + jnp.concatenate(adds, axis=1)
    out[...] = total


def assemble(info, rowi, rowv, colj, colv, parent, rows, cols, inv, pieces):
    def panel_spec(m):
        def index(t, info, rowi, rowv, colj, colv):
            return (info[0] if m == 0 else 1 - info[0], rowi[m, t], 0)

        return pl.BlockSpec((1, NB, PIV), index)

    def block_spec(m, place, u, offset):
        def index(t, info, rowi, rowv, colj, colv):
            here = colj[m, u] // 3 == info[1]
            want = here if place == 0 else jnp.logical_not(here)
            row = rowi[m, t] + (info[0] * 6 if offset else 0)
            return (jnp.where(want, row, 0), jnp.where(want, colj[m, u] % 3, 0))

        return pl.BlockSpec((NB, NB), index)

    specs, operands = [], []
    for m in range(2):
        for place in range(2):
            for u in range(4):
                specs.append(block_spec(m, place, u, m == 0 and place == 0))
                operands.append(pieces[m][place])
    whole = pl.BlockSpec(memory_space=pltpu.VMEM)
    grid_spec = pltpu.PrefetchScalarGridSpec(
        num_scalar_prefetch=5,
        grid=(8,),
        in_specs=[
            pl.BlockSpec((NB, 1024), lambda t, *_: (t, 0)),
            panel_spec(0),
            panel_spec(1),
            whole,
            whole,
            *specs,
        ],
        out_specs=pl.BlockSpec((NB, 1024), lambda t, *_: (t, 0)),
        scratch_shapes=[pltpu.VMEM((2, PIV, 1024), jnp.bfloat16)] * 2,
    )
    return pl.pallas_call(
        assemble_kernel,
        grid_spec=grid_spec,
        out_shape=jax.ShapeDtypeStruct((2048, 1024), F32),
        compiler_params=pltpu.CompilerParams(vmem_limit_bytes=56 << 20),
        cost_estimate=pl.CostEstimate(flops=10**10, bytes_accessed=1 << 25, transcendentals=0),
        name="assemble",
    )(info, rowi, rowv, colj, colv, parent, rows, rows, cols, inv, *operands)


def finish_kernel(info, front, rows, cols, inv, out, high, low):
    t = pl.program_id(0)

    @pl.when(t == 0)
    def _():
        for u in range(4):
            span = slice(u * NB, (u + 1) * NB)
            sh, sl = split(nn(inv[...], cols[:, span]))
            high[:, span] = sh
            low[:, span] = sl

    solved = nt(rows[...], inv[...])
    total = front[...] - dot3(split(solved), (high[...], low[...]))
    in_pivots = (info[0] == 0) & (t < 2)
    wide = lax.broadcasted_iota(jnp.int32, total.shape, 0)
    total = jnp.where(in_pivots & (wide >= 0), 0.0, total)
    row_ids = t * NB + lax.broadcasted_iota(jnp.int32, solved.shape, 0)
    col_ids = lax.broadcasted_iota(jnp.int32, solved.shape, 1)
    factor = jnp.where(in_pivots & (col_ids > row_ids), 0.0, solved)
    lead = jnp.where((info[1] == 0) & (col_ids >= 0), factor, total[:, :PIV])
    out[:, :PIV] = lead
    out[:, PIV:] = total[:, PIV:]


def finish(info, front, rows, cols, inv):
    whole = pl.BlockSpec(memory_space=pltpu.VMEM)
    grid_spec = pltpu.PrefetchScalarGridSpec(
        num_scalar_prefetch=1,
        grid=(8,),
        in_specs=[
            pl.BlockSpec((NB, 1024), lambda t, *_: (t, 0)),
            pl.BlockSpec((NB, PIV), lambda t, *_: (t, 0)),
            whole,
            whole,
        ],
        out_specs=pl.BlockSpec((NB, 1024), lambda t, *_: (t, 0)),
        scratch_shapes=[pltpu.VMEM((PIV, 1024), jnp.bfloat16)] * 2,
    )
    return pl.pallas_call(
        finish_kernel,
        grid_spec=grid_spec,
        out_shape=jax.ShapeDtypeStruct((2048, 1024), F32),
        compiler_params=pltpu.CompilerParams(vmem_limit_bytes=56 << 20),
        cost_estimate=pl.CostEstimate(flops=10**10, bytes_accessed=1 << 25, transcendentals=0),
        name="finish",
    )(info, front, rows, cols, inv)


def inverse_map(targets, first, places, base):
    blocks = first + jnp.arange(6, dtype=jnp.int32)
    usable = blocks >= PIV // NB
    wanted = jnp.clip(blocks - PIV // NB, 0, targets.shape[0] - 1)
    known = jnp.arange(targets.shape[0], dtype=jnp.int32)
    target = jnp.sum(jnp.where(known[None, :] == wanted[:, None], targets[None, :], 0), axis=1)
    hit = usable[:, None] & (target[:, None] == places[None, :])
    index = jnp.sum(jnp.where(hit, jnp.arange(6, dtype=jnp.int32)[:, None], 0), axis=0)
    return index.astype(jnp.int32), jnp.any(hit, axis=0).astype(jnp.int32)


def local(children, parent, relay_map):
    r = lax.axis_index("row")
    c = lax.axis_index("col")
    parity = r % 2
    g, h = c // 2, c % 2
    pair_rows = [(i, i ^ 1) for i in range(8)]
    pair_cols = [(i, i ^ 1) for i in range(16)]

    kept = lax.dynamic_slice_in_dim(children, parity * 1536, 1536, 0)
    leaving = lax.dynamic_slice_in_dim(children, (1 - parity) * 1536, 1536, 0)
    received = lax.ppermute(leaving, "row", pair_rows)
    kept_over = lax.ppermute(kept, "col", pair_cols)

    inverse = leading_inverse(children)
    rows, cols, inv = share_panels(2, children, inverse, 96, 0)
    received_over = lax.ppermute(received, "col", pair_cols)

    row_places = r * 8 + jnp.arange(8, dtype=jnp.int32)
    col_places = c * 4 + jnp.arange(4, dtype=jnp.int32)
    own_map = jnp.where(parity == 0, relay_map[0], relay_map[1])
    other_map = jnp.where(parity == 0, relay_map[1], relay_map[0])
    own_r = inverse_map(own_map, r * 6, row_places, 0)
    other_r = inverse_map(other_map, r * 6, row_places, 0)
    own_c = inverse_map(own_map, g * 6, col_places, 0)
    other_c = inverse_map(other_map, g * 6, col_places, 0)
    rowi, rowv = (jnp.stack(pair) for pair in zip(own_r, other_r))
    colj, colv = (jnp.stack(pair) for pair in zip(own_c, other_c))
    info = jnp.stack([parity, h]).astype(jnp.int32)
    front = assemble(
        info,
        rowi,
        rowv,
        colj,
        colv,
        parent,
        rows,
        cols,
        inv,
        ((children, kept_over), (received, received_over)),
    )

    inv_part = lax.dynamic_slice_in_dim(inv, c * 32, 32, 1)
    factors = jnp.einsum("kic,kjc->kij", rows, inv_part, precision=HI)
    mine = lax.dynamic_index_in_dim(factors, parity, 0, keepdims=False)
    theirs = lax.dynamic_index_in_dim(factors, 1 - parity, 0, keepdims=False)
    mates = lax.ppermute(theirs, "row", pair_rows)
    child_factor = jnp.where(
        parity == 0, jnp.concatenate([mine, mates]), jnp.concatenate([mates, mine])
    )
    row_ids = r // 2 * 3072 + jnp.arange(3072, dtype=jnp.int32)
    col_ids = c * 32 + jnp.arange(32, dtype=jnp.int32)
    child_factor = jnp.where(row_ids[:, None] >= col_ids[None, :], child_factor, 0.0)

    inverse = leading_inverse(front)
    rows, cols, inv = share_panels(1, front, inverse, 128, 1)
    place = jnp.stack([r, c]).astype(jnp.int32)
    parent_out = finish(place, front, rows[0], lax.dynamic_index_in_dim(cols[:, 0], h, 0, False), inv[0])
    return parent_out, child_factor


def solution(mesh):
    return jax.shard_map(
        local,
        mesh=mesh,
        in_specs=(P("row", "col"), P("row", "col"), P()),
        out_specs=(P("row", "col"), P("row", "col")),
        check_vma=False,
    )
```

```python
import jax
import jax.numpy as jnp
from jax import lax
from jax.experimental import pallas as pl
from jax.experimental.pallas import tpu as pltpu
from jax.sharding import PartitionSpec as P

NB = 256
PIV = 512
HI = lax.Precision.HIGHEST
MESH = pl.DeviceIdType.MESH
F32 = jnp.float32


def nt(a, b):
    return lax.dot_general(a, b, (((1,), (1,)), ((), ())), precision=HI, preferred_element_type=jnp.float32)

def nn(a, b):
    return lax.dot_general(a, b, (((1,), (0,)), ((), ())), precision=HI, preferred_element_type=jnp.float32)

def diag_inverse(work, s):
    tiles = [work[pl.ds(s + 8 * t, 8), pl.ds(s, 128)] for t in range(16)]
    rows8 = lax.broadcasted_iota(jnp.int32, (8, 128), 0)
    lanes = lax.broadcasted_iota(jnp.int32, (8, 128), 1)
    unit = [jnp.where(rows8 + 8 * t == lanes, 1.0, 0.0) for t in range(16)]
    scales = [jnp.zeros((8, 1), jnp.float32) for t in range(16)]
    for j in range(128):
        tj, i = j // 8, j % 8
        pivot = tiles[tj][i:i + 1, j:j + 1]
        inv = 1.0 / pivot
        row = tiles[tj][i:i + 1, :] * inv
        mrow = unit[tj][i:i + 1, :] * inv
        for t in range(tj, 16):
            col = tiles[t][:, j:j + 1]
            if t == tj:
                col = jnp.where(rows8[:, :1] > i, col, 0.0)
            tiles[t] = tiles[t] - col * row
            unit[t] = unit[t] - col * mrow
    out = []
    for t in range(16):
        d = jnp.sum(jnp.where(rows8 + 8 * t == lanes, tiles[t], 0.0), axis=1, keepdims=True)
        out.append(unit[t] * lax.rsqrt(d))
    return jnp.concatenate(out, axis=0)

def start_factor(low, inv):
    inv[...] = jnp.zeros_like(inv)
    low[...] = jnp.zeros_like(low)


def factor_step(b, work, low, inv):
    s = pl.multiple_of(b * 128, 128)
    span = pl.ds(s, 128)
    d = diag_inverse(work, s)
    ids = lax.broadcasted_iota(jnp.int32, (PIV, 128), 0)
    beneath = jnp.where(ids >= s + 128, nt(work[:, span], d), 0.0)
    left = nn(low[span, :], inv[...])
    inv[span, :] = -nn(d, left)
    inv[span, span] = d
    low[:, span] = beneath
    work[...] = work[...] - nt(beneath, beneath)


def send(src, dst, send_sem, recv_sem, **device):
    return pltpu.make_async_remote_copy(
        src_ref=src,
        dst_ref=dst,
        send_sem=send_sem,
        recv_sem=recv_sem,
        device_id=device,
        device_id_type=MESH,
    )


def share_kernel(members, moves, *refs):
    src = refs[0]
    refs = refs[1:]
    extra_in, refs = refs[: moves.inputs], refs[moves.inputs :]
    (cols, rows, inv), refs = refs[:3], refs[3:]
    extra_out, refs = refs[: moves.outputs], refs[moves.outputs :]
    work, low, made, diag_sem, here, *sems = refs
    (col_put, col_got, col_out, col_in, col_over) = sems[:5]
    (row_put, row_got, row_out, row_in, row_over) = sems[5:10]
    (inv_put, inv_got, inv_down, inv_down_got, inv_out, inv_in, inv_over) = sems[10:17]
    move_sems = sems[17:]

    r = lax.axis_index("row")
    c = lax.axis_index("col")
    g, h = c // 2, c % 2
    other = c + 1 - 2 * h
    mate = r + 1 - 2 * (r % 2)
    strip = PIV // 8
    giver = r < members
    root = giver & (c == 0)
    home = giver & (g == r)

    barrier = pltpu.get_barrier_semaphore()
    for d in range(1, 8):
        pl.semaphore_signal(barrier, 1, device_id={"row": (r + d) % 8}, device_id_type=MESH)
    for d in range(1, 16):
        pl.semaphore_signal(barrier, 1, device_id={"col": (c + d) % 16}, device_id_type=MESH)
    for k in range(members):

        @pl.when(jnp.logical_not((r == k) & (g == r)))
        def _():
            pl.semaphore_signal(
                barrier, 1, device_id={"row": k, "col": 2 * r + h}, device_id_type=MESH
            )

    @pl.when(giver)
    def _():
        for d in range(8):

            @pl.when(jnp.logical_not((g == r) & (g == d)))
            def _():
                pl.semaphore_signal(
                    barrier, 1, device_id={"row": g, "col": 2 * d + h}, device_id_type=MESH
                )

    count = 22 + members + jnp.where(giver, 8, 0) - jnp.where(home, 2, 0)
    pl.semaphore_wait(barrier, count)

    def part(index):
        return pl.ds(pl.multiple_of(index * strip, strip), strip)

    def slot(buffer, k, index, half=None):
        return buffer.at[h if half is None else half, k, part(index), :]

    def col_scatter(k, d):
        dest = (r + d) % 8
        return send(
            src.at[part(dest), :],
            slot(cols, k, dest),
            col_put.at[d],
            col_got.at[k],
            row=dest,
            col=c,
        )

    def row_scatter(k, dest):
        return send(
            src.at[part(dest), :],
            slot(rows, k, dest),
            row_put.at[dest],
            row_got.at[k],
            row=g,
            col=2 * dest + h,
        )

    def row_taken(k):
        return send(
            slot(rows, k, g), slot(rows, k, g), row_put.at[0], row_got.at[k], row=r, col=other
        )

    def inv_scatter(k, d):
        dest = (c + d) % 16
        at = (dest % 2 * 8 + dest // 2) * 32
        return send(
            made.at[pl.ds(pl.multiple_of(at, 32), 32), :],
            inv.at[k, dest % 2, dest // 2],
            inv_put.at[d],
            inv_got.at[k],
            row=r,
            col=dest,
        )

    local_diag = pltpu.make_async_copy(src.at[pl.ds(0, PIV), pl.ds(0, PIV)], work, diag_sem.at[0])
    local_col = pltpu.make_async_copy(src.at[part(r), :], slot(cols, r, r), here.at[1])
    local_row = pltpu.make_async_copy(src.at[part(g), :], slot(rows, r, g), here.at[0])
    local_inv = pltpu.make_async_copy(made.at[pl.ds(0, 32), :], inv.at[r, 0, 0], here.at[2])

    @pl.when(root)
    def _():
        local_diag.start()

    @pl.when(giver)
    def _():
        local_col.start()

        @pl.loop(1, 8)
        def _(d):
            col_scatter(r, d).start()

        @pl.loop(0, 8)
        def _(d):
            @pl.when(jnp.logical_not((g == r) & (g == d)))
            def _():
                row_scatter(r, d).start()

        @pl.when(home)
        def _():
            local_row.start()

    def block_move(index, relay=False):
        return moves.copy(index, relay, extra_in, extra_out, move_sems, send, r, c, h, mate, other)

    for index in range(moves.count):
        block_move(index).start()

    @pl.when(root)
    def _():
        local_diag.wait()
        start_factor(low, made)
        factor_step(0, work, low, made)

    def col_gather(k, d, sender=None):
        at = r if sender is None else sender
        return send(
            slot(cols, k, at),
            slot(cols, k, at),
            col_out.at[k, d],
            col_in.at[k, at],
            row=(r + d) % 8,
            col=c,
        )

    def row_gather(k, d, sender=None):
        at = g if sender is None else sender
        return send(
            slot(rows, k, at),
            slot(rows, k, at),
            row_out.at[k, d],
            row_in.at[k, at],
            row=r,
            col=(g + d) % 8 * 2 + h,
        )

    def inv_column(k, d):
        return send(
            inv.at[k, h, g],
            inv.at[k, h, g],
            inv_down.at[d],
            inv_down_got.at[k],
            row=(r + d) % 8,
            col=c,
        )

    def inv_gather(k, d, sender=None):
        at = g if sender is None else sender
        return send(
            inv.at[k, h, at],
            inv.at[k, h, at],
            inv_out.at[k, d],
            inv_in.at[k, at],
            row=r,
            col=(g + d) % 8 * 2 + h,
        )

    for k in range(members):

        @pl.when(r == k)
        def _():
            local_col.wait()

        @pl.when(r != k)
        def _():
            col_scatter(k, 1).wait_recv()

        @pl.loop(1, 8)
        def _(d):
            col_gather(k, d).start()

        @pl.when((r == k) & (g == r))
        def _():
            local_row.wait()

        @pl.when(jnp.logical_not((r == k) & (g == r)))
        def _():
            row_taken(k).wait_recv()

        @pl.loop(1, 8)
        def _(d):
            row_gather(k, d).start()

    @pl.when(root)
    def _():
        @pl.loop(1, 4)
        def _(b):
            factor_step(b, work, low, made)

        local_inv.start()

        @pl.loop(1, 16)
        def _(d):
            inv_scatter(r, d).start()

        local_inv.wait()

    def cross(buffer, sems):
        return send(buffer, buffer, sems.at[0], sems.at[1], row=r, col=other)

    if members == 2:
        for k in range(members):

            @pl.loop(1, 8)
            def _(d):
                col_gather(k, d, (r + d) % 8).wait_recv()

        cross(cols.at[h], col_over).start()
    for k in range(members):

        @pl.loop(1, 8)
        def _(d):
            row_gather(k, d, (g + d) % 8).wait_recv()

    cross(rows.at[h], row_over).start()

    for k in range(members):

        @pl.when((r == k) & (c != 0))
        def _():
            inv_scatter(k, 1).wait_recv()

        @pl.when(r == k)
        def _():
            @pl.loop(1, 8)
            def _(d):
                inv_column(k, d).start()

    for k in range(members):

        @pl.when(r != k)
        def _():
            inv_column(k, 1).wait_recv()

        @pl.loop(1, 8)
        def _(d):
            inv_gather(k, d).start()

    for index in range(moves.relayed):
        block_move(index).wait_recv()
        block_move(index, True).start()

    for k in range(members):

        @pl.loop(1, 8)
        def _(d):
            inv_gather(k, d, (g + d) % 8).wait_recv()

        cross(inv.at[k, h], inv_over.at[k]).start()

    if members == 1:

        @pl.loop(1, 8)
        def _(d):
            col_gather(0, d, (r + d) % 8).wait_recv()

    if members == 2:
        cross(cols.at[1 - h], col_over).wait_recv()
        cross(cols.at[h], col_over).wait_send()
    cross(rows.at[1 - h], row_over).wait_recv()
    cross(rows.at[h], row_over).wait_send()
    for index in range(moves.count):
        if index >= moves.relayed:
            block_move(index).wait_recv()
        block_move(index).wait_send()
        if index < moves.relayed:
            block_move(index, True).wait()
    for k in range(members):
        cross(inv.at[k, 1 - h], inv_over.at[k]).wait_recv()
        cross(inv.at[k, h], inv_over.at[k]).wait_send()

        @pl.loop(1, 8)
        def _(d):
            col_gather(k, d).wait_send()
            row_gather(k, d).wait_send()
            inv_gather(k, d).wait_send()

        @pl.when(r == k)
        def _():
            @pl.loop(1, 8)
            def _(d):
                col_scatter(k, d).wait_send()
                inv_column(k, d).wait_send()

            @pl.loop(0, 8)
            def _(d):
                @pl.when(jnp.logical_not((g == r) & (g == d)))
                def _():
                    row_scatter(k, d).wait_send()

        @pl.when((r == k) & (c == 0))
        def _():
            @pl.loop(1, 16)
            def _(d):
                inv_scatter(k, d).wait_send()


class EarlyMoves:
    inputs, outputs = 0, 2
    relayed = 4
    count = 5

    def copy(self, index, relay, ins, outs, sems, send, r, c, h, mate, other):
        (got, kept), (put_sem, got_sem, over_put, over_got) = outs, sems
        src = self.src
        if index == 4:
            rows = pl.ds(pl.multiple_of(r % 2 * 1536, NB), 1536)
            return send(src.at[rows, :], kept, put_sem.at[4], got_sem.at[4], row=r, col=other)
        if relay:
            block = got.at[h, pl.ds(index * NB, NB), :]
            return send(block, block, over_put.at[index], over_got.at[index], row=r, col=other)
        rows = pl.ds(pl.multiple_of((1 - r % 2) * 1536 + (index + 2) * NB, NB), NB)
        return send(
            src.at[rows, :],
            got.at[h, pl.ds(index * NB, NB), :],
            put_sem.at[index],
            got_sem.at[index],
            row=mate,
            col=c,
        )


class LateMoves:
    inputs, outputs = 2, 2
    relayed = 2
    count = 3

    def copy(self, index, relay, ins, outs, sems, send, r, c, h, mate, other):
        (children, factors), (got, mates), (put_sem, got_sem, over_put, over_got) = ins, outs, sems
        if index == 2:
            return send(
                factors.at[1 - r % 2], mates, put_sem.at[2], got_sem.at[2], row=mate, col=c
            )
        if relay:
            block = got.at[h, pl.ds(index * NB, NB), :]
            return send(block, block, over_put.at[index], over_got.at[index], row=r, col=other)
        rows = pl.ds(pl.multiple_of((1 - r % 2) * 1536 + index * NB, NB), NB)
        return send(
            children.at[rows, :],
            got.at[h, pl.ds(index * NB, NB), :],
            put_sem.at[index],
            got_sem.at[index],
            row=mate,
            col=c,
        )


def share(members, source, extras, moves, extra_shapes, collective_id):
    width = source.shape[1]
    dma = pltpu.SemaphoreType.DMA
    panel = jax.ShapeDtypeStruct((2, members, PIV, width), F32)
    out_shape = (panel, panel, jax.ShapeDtypeStruct((members, 2, 8, 32, PIV), F32), *extra_shapes)
    group = [dma((8,)), dma((members,)), dma((members, 8)), dma((members, 8)), dma((2,))]
    scratch = [
        pltpu.VMEM((PIV, PIV), F32),
        pltpu.VMEM((PIV, PIV), F32),
        pltpu.VMEM((PIV, PIV), F32),
        dma((1,)),
        dma((3,)),
        *group,
        *group,
        dma((16,)),
        dma((members,)),
        dma((8,)),
        dma((members,)),
        dma((members, 8)),
        dma((members, 8)),
        dma((members, 2)),
        dma((moves.count,)),
        dma((moves.count,)),
        dma((moves.relayed,)),
        dma((moves.relayed,)),
    ]

    def kernel(*refs):
        if members == 2:
            moves.src = refs[0]
        share_kernel(members, moves, *refs)

    cols, rows, inv, *extra = pl.pallas_call(
        kernel,
        out_shape=out_shape,
        in_specs=[pl.BlockSpec(memory_space=pl.ANY)] * (1 + len(extras)),
        out_specs=[pl.BlockSpec(memory_space=pl.ANY)] * len(out_shape),
        scratch_shapes=scratch,
        compiler_params=pltpu.CompilerParams(
            collective_id=collective_id, has_side_effects=True, vmem_limit_bytes=56 << 20
        ),
        cost_estimate=pl.CostEstimate(flops=10**10, bytes_accessed=1 << 25, transcendentals=0),
        name="share_panels_%d" % members,
    )(source, *extras)
    return cols, rows, inv.reshape(members, PIV, PIV), extra


def split(value):
    high = value.astype(jnp.bfloat16)
    return high, (value - high.astype(F32)).astype(jnp.bfloat16)


def dot3(left, right):
    (lh, ll), (rh, rl) = left, right

    def one(a, b):
        return jnp.dot(a, b, preferred_element_type=F32)

    return one(lh, rh) + (one(lh, rl) + one(ll, rh))


def column_block(panels, k, block):
    at = pl.multiple_of(block % 3 * NB, NB)
    return panels[block // 3, k, :, pl.ds(at, NB)]


def update_blocks(t, info, rowi, rowv, colj, colv, blocks):
    total = None
    for m in range(2):
        adds = []
        for u in range(4):
            first, second = blocks[m * 8 + u], blocks[m * 8 + 4 + u]
            use = (rowv[m, t] > 0) & (colv[m, u] > 0)
            if m == 0:
                block = jnp.where(colj[m, u] // 3 == info[1], first[...], second[...])
            else:
                block = jnp.where(rowi[m, t] >= 2, first[0], second[0])
            adds.append(jnp.where(use, block, 0.0))
        sum_m = jnp.concatenate(adds, axis=1)
        total = sum_m if total is None else total + sum_m
    return total


def block_specs():
    def own(u, place):
        def index(t, info, rowi, rowv, colj, colv):
            here = colj[0, u] // 3 == info[1]
            want = here if place == 0 else jnp.logical_not(here)
            row = rowi[0, t] + (info[0] * 6 if place == 0 else 0)
            return (jnp.where(want, row, 0), jnp.where(want, colj[0, u] % 3, 0))

        return pl.BlockSpec((NB, NB), index)

    def mates(u, place):
        def index(t, info, rowi, rowv, colj, colv):
            late = rowi[1, t] < 2
            want = jnp.logical_not(late) if place == 0 else late
            row = rowi[1, t] - (2 if place == 0 else 0)
            core = colj[1, u] // 3
            return (core, jnp.where(want, row, 0), jnp.where(want, colj[1, u] % 3, 0))

        return pl.BlockSpec((1, NB, NB), index)

    return [own(u, place) for place in range(2) for u in range(4)] + [
        mates(u, place) for place in range(2) for u in range(4)
    ]


def panel_kernel(info, rowi, rowv, colj, colv, parent, rows, cols, inv, inv_part, *rest):
    blocks, (front, high, low, factors), (inv_h, inv_l) = rest[:16], rest[16:20], rest[20:]
    t = pl.program_id(0)

    @pl.when(t == 0)
    def _():
        for k in range(2):
            inv_h[k], inv_l[k] = split(inv[k])
        for m in range(2):
            k = info[0] if m == 0 else 1 - info[0]
            for u in range(4):
                block = split(column_block(cols, k, colj[m, u]))
                solved = dot3((inv_h[k], inv_l[k]), block)
                solved = jnp.where(colv[m, u] > 0, solved, 0.0)
                sh, sl = split(solved)
                high[m, :, u * NB : (u + 1) * NB] = sh
                low[m, :, u * NB : (u + 1) * NB] = sl
        for k in range(2):
            part = split(inv_part[k])
            for half in range(2):
                factors[k, :, half * 768 : (half + 1) * 768] = dot3(part, split(rows[half, k]))

    total = parent[...] + update_blocks(t, info, rowi, rowv, colj, colv, blocks)
    for m in range(2):
        k = info[0] if m == 0 else 1 - info[0]
        block = split(column_block(rows, k, rowi[m, t]))
        solved = dot3((inv_h[k], inv_l[k]), block)
        solved = jnp.where(rowv[m, t] > 0, solved, 0.0)
        total = total - dot3(split(solved.T), (high[m], low[m]))
    front[...] = total


def panel_front(maps, parent, rows, cols, inv, inv_part, pieces):
    whole = pl.BlockSpec(memory_space=pltpu.VMEM)
    full = lambda shape: pl.BlockSpec(shape, lambda t, *_: (0,) * len(shape))
    grid_spec = pltpu.PrefetchScalarGridSpec(
        num_scalar_prefetch=5,
        grid=(2,),
        in_specs=[
            pl.BlockSpec((NB, 1024), lambda t, *_: (t, 0)),
            whole,
            whole,
            whole,
            whole,
            *block_specs(),
        ],
        out_specs=[
            pl.BlockSpec((NB, 1024), lambda t, *_: (t, 0)),
            full((2, PIV, 1024)),
            full((2, PIV, 1024)),
            full((2, 32, 1536)),
        ],
        scratch_shapes=[pltpu.VMEM((2, PIV, PIV), jnp.bfloat16)] * 2,
    )
    return pl.pallas_call(
        panel_kernel,
        grid_spec=grid_spec,
        out_shape=(
            jax.ShapeDtypeStruct((PIV, 1024), F32),
            jax.ShapeDtypeStruct((2, PIV, 1024), jnp.bfloat16),
            jax.ShapeDtypeStruct((2, PIV, 1024), jnp.bfloat16),
            jax.ShapeDtypeStruct((2, 32, 1536), F32),
        ),
        compiler_params=pltpu.CompilerParams(vmem_limit_bytes=56 << 20),
        cost_estimate=pl.CostEstimate(flops=10**10, bytes_accessed=1 << 25, transcendentals=0),
        name="panel_front",
    )(*maps, parent, rows, cols, inv, inv_part, *pieces)


def finish_kernel(info, rowi, rowv, colj, colv, parent, rows, inv, front, prows, pinv, *rest):
    (high, low), blocks, out = rest[:2], rest[2:18], rest[18]
    inv_h, inv_l, par_h, par_l = rest[19:]
    t = pl.program_id(0)

    @pl.when(t == 0)
    def _():
        for k in range(2):
            inv_h[k], inv_l[k] = split(inv[k])
        inv_h[2], inv_l[2] = split(pinv[...])
        for u in range(4):
            span = slice(u * NB, (u + 1) * NB)
            par_h[:, span], par_l[:, span] = split(
                dot3((inv_h[2], inv_l[2]), split(front[0, :, span]))
            )

    total = parent[...] + update_blocks(t, info, rowi, rowv, colj, colv, blocks)
    for m in range(2):
        k = info[0] if m == 0 else 1 - info[0]
        block = split(column_block(rows, k, rowi[m, t]))
        solved = dot3((inv_h[k], inv_l[k]), block)
        solved = jnp.where(rowv[m, t] > 0, solved, 0.0)
        total = total - dot3(split(solved.T), (high[m], low[m]))
    block = split(prows[0])
    solved = dot3((inv_h[2], inv_l[2]), block).T
    total = total - dot3(split(solved), (par_h[...], par_l[...]))
    in_pivots = (info[2] == 0) & (t < 2)
    wide = lax.broadcasted_iota(jnp.int32, total.shape, 0)
    total = jnp.where(in_pivots & (wide >= 0), 0.0, total)
    row_ids = t * NB + lax.broadcasted_iota(jnp.int32, solved.shape, 0)
    col_ids = lax.broadcasted_iota(jnp.int32, solved.shape, 1)
    factor = jnp.where(in_pivots & (col_ids > row_ids), 0.0, solved)
    lead = jnp.where((info[3] == 0) & (col_ids >= 0), factor, total[:, :PIV])
    out[:, :PIV] = lead
    out[:, PIV:] = total[:, PIV:]


def finish(maps, parent, rows, inv, front_cols, front_rows, front_inv, high, low, pieces):
    whole = pl.BlockSpec(memory_space=pltpu.VMEM)
    grid_spec = pltpu.PrefetchScalarGridSpec(
        num_scalar_prefetch=5,
        grid=(8,),
        in_specs=[
            pl.BlockSpec((NB, 1024), lambda t, *_: (t, 0)),
            whole,
            whole,
            pl.BlockSpec((1, PIV, 1024), lambda t, info, *_: (info[1], 0, 0)),
            pl.BlockSpec((1, PIV, NB), lambda t, *_: (t // 4, 0, t % 4)),
            whole,
            whole,
            whole,
            *block_specs(),
        ],
        out_specs=pl.BlockSpec((NB, 1024), lambda t, *_: (t, 0)),
        scratch_shapes=[
            *[pltpu.VMEM((3, PIV, PIV), jnp.bfloat16)] * 2,
            *[pltpu.VMEM((PIV, 1024), jnp.bfloat16)] * 2,
        ],
    )
    return pl.pallas_call(
        finish_kernel,
        grid_spec=grid_spec,
        out_shape=jax.ShapeDtypeStruct((2048, 1024), F32),
        compiler_params=pltpu.CompilerParams(vmem_limit_bytes=56 << 20),
        cost_estimate=pl.CostEstimate(flops=10**10, bytes_accessed=1 << 25, transcendentals=0),
        name="finish",
    )(*maps, parent, rows, inv, front_cols, front_rows, front_inv, high, low, *pieces)


def inverse_map(targets, first, places):
    blocks = first + jnp.arange(6, dtype=jnp.int32)
    usable = blocks >= PIV // NB
    wanted = jnp.clip(blocks - PIV // NB, 0, targets.shape[0] - 1)
    known = jnp.arange(targets.shape[0], dtype=jnp.int32)
    target = jnp.sum(jnp.where(known[None, :] == wanted[:, None], targets[None, :], 0), axis=1)
    hit = usable[:, None] & (target[:, None] == places[None, :])
    index = jnp.sum(jnp.where(hit, jnp.arange(6, dtype=jnp.int32)[:, None], 0), axis=0)
    return index.astype(jnp.int32), jnp.any(hit, axis=0).astype(jnp.int32)


def local(children, parent, relay_map):
    r = lax.axis_index("row")
    c = lax.axis_index("col")
    parity = r % 2
    g, h = c // 2, c % 2

    row_places = r * 8 + jnp.arange(8, dtype=jnp.int32)
    col_places = c * 4 + jnp.arange(4, dtype=jnp.int32)
    own_map = jnp.where(parity == 0, relay_map[0], relay_map[1])
    other_map = jnp.where(parity == 0, relay_map[1], relay_map[0])
    own_r = inverse_map(own_map, r * 6, row_places)
    other_r = inverse_map(other_map, r * 6, row_places)
    own_c = inverse_map(own_map, g * 6, col_places)
    other_c = inverse_map(other_map, g * 6, col_places)
    rowi, rowv = (jnp.stack(pair) for pair in zip(own_r, other_r))
    colj, colv = (jnp.stack(pair) for pair in zip(own_c, other_c))
    info = jnp.stack([parity, h, r, c]).astype(jnp.int32)
    maps = (info, rowi, rowv, colj, colv)

    shape = jax.ShapeDtypeStruct
    cols, rows, inv, (early, kept) = share(
        2, children, (), EarlyMoves(), (shape((2, 1024, 768), F32), shape((1536, 768), F32)), 0
    )
    inv_part = lax.dynamic_slice_in_dim(inv, c * 32, 32, 1)
    pieces = [children] * 4 + [kept] * 4 + [early] * 4
    front, high, low, factors = panel_front(
        maps, parent, rows, cols, inv, inv_part, pieces + [early] * 4
    )
    front_cols, front_rows, front_inv, (late, mates) = share(
        1,
        front,
        (children, factors),
        LateMoves(),
        (shape((2, 512, 768), F32), shape((32, 1536), F32)),
        1,
    )
    parent_out = finish(
        maps,
        parent,
        rows,
        inv,
        front_cols[:, 0],
        front_rows[:, 0],
        front_inv[0],
        high,
        low,
        pieces + [late] * 4,
    )
    mine = lax.dynamic_index_in_dim(factors, parity, 0, keepdims=False)
    first = jnp.where(parity == 0, mine, mates)
    second = jnp.where(parity == 0, mates, mine)
    child_factor = jnp.concatenate([first, second], axis=1).T
    row_ids = r // 2 * 3072 + jnp.arange(3072, dtype=jnp.int32)
    col_ids = c * 32 + jnp.arange(32, dtype=jnp.int32)
    child_factor = jnp.where(row_ids[:, None] >= col_ids[None, :], child_factor, 0.0)
    return parent_out, child_factor


def solution(mesh):
    return jax.shard_map(
        local,
        mesh=mesh,
        in_specs=(P("row", "col"), P("row", "col"), P()),
        out_specs=(P("row", "col"), P("row", "col")),
        check_vma=False,
    )
```

```python
import jax
import jax.numpy as jnp
from jax import lax
from jax.experimental import pallas as pl
from jax.experimental.pallas import tpu as pltpu
from jax.sharding import PartitionSpec as P

NB = 256
PIV = 512
HI = lax.Precision.HIGHEST
MESH = pl.DeviceIdType.MESH
F32 = jnp.float32


def nt(a, b):
    return lax.dot_general(a, b, (((1,), (1,)), ((), ())), precision=HI, preferred_element_type=jnp.float32)

def nn(a, b):
    return lax.dot_general(a, b, (((1,), (0,)), ((), ())), precision=HI, preferred_element_type=jnp.float32)

def diag_inverse(work, s):
    tiles = [work[pl.ds(s + 8 * t, 8), pl.ds(s, 128)] for t in range(16)]
    rows8 = lax.broadcasted_iota(jnp.int32, (8, 128), 0)
    lanes = lax.broadcasted_iota(jnp.int32, (8, 128), 1)
    unit = [jnp.where(rows8 + 8 * t == lanes, 1.0, 0.0) for t in range(16)]
    scales = [jnp.zeros((8, 1), jnp.float32) for t in range(16)]
    for j in range(128):
        tj, i = j // 8, j % 8
        pivot = tiles[tj][i:i + 1, j:j + 1]
        inv = 1.0 / pivot
        row = tiles[tj][i:i + 1, :] * inv
        mrow = unit[tj][i:i + 1, :] * inv
        for t in range(tj, 16):
            col = tiles[t][:, j:j + 1]
            if t == tj:
                col = jnp.where(rows8[:, :1] > i, col, 0.0)
            tiles[t] = tiles[t] - col * row
            unit[t] = unit[t] - col * mrow
    out = []
    for t in range(16):
        d = jnp.sum(jnp.where(rows8 + 8 * t == lanes, tiles[t], 0.0), axis=1, keepdims=True)
        out.append(unit[t] * lax.rsqrt(d))
    return jnp.concatenate(out, axis=0)

def start_factor(low, inv):
    inv[...] = jnp.zeros_like(inv)
    low[...] = jnp.zeros_like(low)


def factor_step(b, work, low, inv):
    s = pl.multiple_of(b * 128, 128)
    span = pl.ds(s, 128)
    d = diag_inverse(work, s)
    ids = lax.broadcasted_iota(jnp.int32, (PIV, 128), 0)
    beneath = jnp.where(ids >= s + 128, nt(work[:, span], d), 0.0)
    left = nn(low[span, :], inv[...])
    inv[span, :] = -nn(d, left)
    inv[span, span] = d
    low[:, span] = beneath
    work[...] = work[...] - nt(beneath, beneath)


def send(src, dst, send_sem, recv_sem, **device):
    return pltpu.make_async_remote_copy(
        src_ref=src,
        dst_ref=dst,
        send_sem=send_sem,
        recv_sem=recv_sem,
        device_id=device,
        device_id_type=MESH,
    )


def share_kernel(members, moves, *refs):
    src = refs[0]
    refs = refs[1:]
    extra_in, refs = refs[: moves.inputs], refs[moves.inputs :]
    (cols, rows, inv), refs = refs[:3], refs[3:]
    extra_out, refs = refs[: moves.outputs], refs[moves.outputs :]
    work, low, made, diag_sem, here, *sems = refs
    (col_put, col_got, col_out, col_in, col_swap, col_over) = sems[:6]
    (row_put, row_got, row_swap, row_out, row_in, row_over) = sems[6:12]
    (inv_put, inv_got, inv_down, inv_down_got, inv_out, inv_in, inv_over) = sems[12:19]
    move_sems = sems[19:]

    r = lax.axis_index("row")
    c = lax.axis_index("col")
    g, h = c // 2, c % 2
    other = c + 1 - 2 * h
    mate = r + 1 - 2 * (r % 2)
    strip, quarter = PIV // 8, PIV // 4
    plane, level = r // 4, r % 4
    ring, side = c // 4, c // 2 % 2
    parity = r % 2
    giver = r < members
    root = giver & (c == 0)
    home = giver & (g == r)

    barrier = pltpu.get_barrier_semaphore()

    def greet(row, col):
        pl.semaphore_signal(barrier, 1, device_id={"row": row, "col": col}, device_id_type=MESH)

    for d in range(1, 4):
        greet(plane * 4 + (level + d) % 4, c)
    greet((1 - plane) * 4 + level, c)
    for d in range(1, 8):
        greet(r, (g + d) % 8 * 2 + h)
    greet(r, other)
    for k in range(members):
        pl.when(r != k)(lambda k=k: greet(k, c))
    if members == 2:
        pl.when(c != 0)(lambda: greet(r, 0))
        greet(mate, 0)
        count = 12 + jnp.where(giver, 7, 0) + jnp.where(c == 0, 31, 0)
    else:
        pl.when(jnp.logical_not(home))(lambda: greet(0, 2 * r + h))
        pl.when(giver & (c != 0))(lambda: greet(0, 0))
        count = 12 + jnp.where(giver, 15, 0) - jnp.where(home, 1, 0) + jnp.where(root, 15, 0)
    pl.semaphore_wait(barrier, count)

    def part(index):
        return pl.ds(pl.multiple_of(index * strip, strip), strip)

    def slot(k, index):
        return cols.at[h, k, part(index), :]

    def row_slot(k, index):
        return rows.at[k, h, index] if members == 2 else rows.at[h, k, part(index), :]

    def col_scatter(k, d):
        dest = (r + d) % 8
        return send(
            src.at[part(dest), :],
            slot(k, dest),
            col_put.at[d],
            col_got.at[k],
            row=dest,
            col=c,
        )

    def row_piece(target, dest):
        start = target % 2 * 1536 + (dest % 2 * 8 + dest // 2) * 96
        return src.at[pl.ds(pl.multiple_of(start, 32), 96), pl.ds(0, PIV)]

    def row_scatter(d, to_mate=False):
        if members == 2:
            dest = (c + d) % 16
            target = mate if to_mate else r
            return send(
                row_piece(target, dest),
                rows.at[parity, dest % 2, dest // 2],
                row_put.at[1 if to_mate else 0, d],
                row_got.at[parity],
                row=target,
                col=dest,
            )
        return send(
            src.at[part(d), :],
            row_slot(0, d),
            row_put.at[0, d],
            row_got.at[0],
            row=g,
            col=2 * d + h,
        )

    def row_taken(k):
        return send(
            row_slot(k, g), row_slot(k, g), row_put.at[0, 0], row_got.at[k], row=r, col=other
        )

    def inv_scatter(k, d):
        dest = (c + d) % 16
        at = (dest % 2 * 8 + dest // 2) * 32
        return send(
            made.at[pl.ds(pl.multiple_of(at, 32), 32), :],
            inv.at[k, dest % 2, dest // 2],
            inv_put.at[d],
            inv_got.at[k],
            row=r,
            col=dest,
        )

    local_diag = pltpu.make_async_copy(src.at[pl.ds(0, PIV), pl.ds(0, PIV)], work, diag_sem.at[0])
    local_col = pltpu.make_async_copy(src.at[part(r), :], slot(r, r), here.at[1])
    local_row = pltpu.make_async_copy(
        row_piece(r, 0) if members == 2 else src.at[part(g), :],
        row_slot(parity if members == 2 else 0, g),
        here.at[0],
    )
    local_inv = pltpu.make_async_copy(made.at[pl.ds(0, 32), :], inv.at[r, 0, 0], here.at[2])

    @pl.when(root)
    def _():
        local_diag.start()

    @pl.when(giver)
    def _():
        local_col.start()

        @pl.loop(1, 8)
        def _(d):
            col_scatter(r, d).start()

    if members == 2:

        @pl.when(c == 0)
        def _():
            local_row.start()

            @pl.loop(1, 16)
            def _(d):
                row_scatter(d).start()

            row_scatter(0, True).start()

            @pl.loop(1, 16)
            def _(d):
                row_scatter(d, True).start()

    else:

        @pl.when(giver)
        def _():
            @pl.loop(0, 8)
            def _(d):
                @pl.when(jnp.logical_not(home & (g == d)))
                def _():
                    row_scatter(d).start()

        @pl.when(home)
        def _():
            local_row.start()

    block_move, aside = moves.copies(extra_in, extra_out, move_sems, src, r, c, h, mate, other)

    def each_block(act):
        for index in range(6):
            pl.when(moves.sends(r, index))(lambda index=index: act(index))

    @pl.when(root)
    def _():
        local_diag.wait()
        start_factor(low, made)
        factor_step(0, work, low, made)

    def col_gather(d, arriving=False):
        peer = (level + d) % 4
        at = plane * 4 + (peer if arriving else level)
        strips = cols.at[h, :, part(at), :]
        return send(
            strips, strips, col_out.at[d], col_in.at[at % 4], row=plane * 4 + peer, col=c
        )

    def col_half(from_plane):
        rows_of = pl.ds(pl.multiple_of(from_plane * NB, NB), NB)
        half = cols.at[h, :, rows_of, :]
        return send(half, half, col_swap.at[0], col_swap.at[1], row=(1 - plane) * 4 + level, col=c)

    pair = c + 2 - 4 * side

    def row_pair(k, arriving=False):
        strips = row_slot(k, g + 1 - 2 * side if arriving else g)
        return send(strips, strips, row_swap.at[0, k], row_swap.at[1, k], row=r, col=pair)

    def row_gather(k, d, arriving=False):
        peer = (ring + d) % 4
        at = peer if arriving else ring
        if members == 2:
            strips = rows.at[k, h, pl.ds(2 * at, 2)]
        else:
            strips = rows.at[h, k, pl.ds(pl.multiple_of(at * 2 * strip, 2 * strip), 2 * strip), :]
        return send(
            strips,
            strips,
            row_out.at[k, d],
            row_in.at[k, at],
            row=r,
            col=peer * 4 + side * 2 + h,
        )

    row_order = (parity, 1 - parity) if members == 2 else (0,)

    def inv_column(k, d):
        return send(
            inv.at[k, h, g],
            inv.at[k, h, g],
            inv_down.at[d],
            inv_down_got.at[k],
            row=(r + d) % 8,
            col=c,
        )

    def inv_gather(d, arriving=False):
        peer = (g + d) % 8
        at = peer if arriving else g
        part_of = inv.at[:, h, at]
        return send(part_of, part_of, inv_out.at[d], inv_in.at[at], row=r, col=peer * 2 + h)

    def cross(buffer, sems):
        return send(buffer, buffer, sems.at[0], sems.at[1], row=r, col=other)

    def row_cross(half):
        return cross(rows.at[:, half] if members == 2 else rows.at[half], row_over)

    for k in range(members):

        @pl.when(r == k)
        def _():
            local_col.wait()

        @pl.when(r != k)
        def _():
            col_scatter(k, 1).wait_recv()

    @pl.loop(1, 4)
    def _(d):
        col_gather(d).start()

    for turn, k in enumerate(row_order):
        holds = (c == 0) & (turn == 0) if members == 2 else home

        @pl.when(holds)
        def _():
            local_row.wait()

        @pl.when(jnp.logical_not(holds))
        def _():
            row_taken(k).wait_recv()

        row_pair(k).start()

    each_block(lambda index: block_move(index).start())
    aside().start()

    @pl.when(root)
    def _():
        @pl.loop(1, 3)
        def _(b):
            factor_step(b, work, low, made)

    for k in row_order:
        row_pair(k, True).wait_recv()

        @pl.loop(1, 4)
        def _(d):
            row_gather(k, d).start()

    @pl.loop(1, 4)
    def _(d):
        col_gather(d, True).wait_recv()

    col_half(plane).start()

    @pl.when(root)
    def _():
        factor_step(3, work, low, made)

        local_inv.start()

        @pl.loop(1, 16)
        def _(d):
            inv_scatter(r, d).start()

        local_inv.wait()

    for k in range(members):

        @pl.when((r == k) & (c != 0))
        def _():
            inv_scatter(k, 1).wait_recv()

        @pl.when(r == k)
        def _():
            @pl.loop(1, 8)
            def _(d):
                inv_column(k, d).start()

    for k in range(members):

        @pl.when(r != k)
        def _():
            inv_column(k, 1).wait_recv()

    @pl.loop(1, 8)
    def _(d):
        inv_gather(d).start()

    col_half(1 - plane).wait_recv()
    if members == 2:
        cross(cols.at[h], col_over).start()

    for k in row_order:

        @pl.loop(1, 4)
        def _(d):
            row_gather(k, d, True).wait_recv()

    row_cross(h).start()

    @pl.loop(1, 8)
    def _(d):
        inv_gather(d, True).wait_recv()

    cross(inv.at[:, h], inv_over).start()

    def pass_on(index):
        block_move(index).wait_recv()
        block_move(index, True).start()

    each_block(pass_on)

    if members == 2:
        cross(cols.at[1 - h], col_over).wait_recv()
        cross(cols.at[h], col_over).wait_send()
    col_half(plane).wait_send()
    row_cross(1 - h).wait_recv()
    row_cross(h).wait_send()
    cross(inv.at[:, 1 - h], inv_over).wait_recv()
    cross(inv.at[:, h], inv_over).wait_send()

    def settle(index):
        block_move(index).wait_send()
        block_move(index, True).wait()

    each_block(settle)
    aside().wait()

    @pl.loop(1, 4)
    def _(d):
        col_gather(d).wait_send()

    @pl.loop(1, 8)
    def _(d):
        inv_gather(d).wait_send()

    for k in row_order:
        row_pair(k).wait_send()

        @pl.loop(1, 4)
        def _(d):
            row_gather(k, d).wait_send()

    for k in range(members):

        @pl.when(r == k)
        def _():
            @pl.loop(1, 8)
            def _(d):
                col_scatter(k, d).wait_send()
                inv_column(k, d).wait_send()

        @pl.when((r == k) & (c == 0))
        def _():
            @pl.loop(1, 16)
            def _(d):
                inv_scatter(k, d).wait_send()

    if members == 2:

        @pl.when(c == 0)
        def _():
            @pl.loop(1, 16)
            def _(d):
                row_scatter(d).wait_send()

            @pl.loop(0, 16)
            def _(d):
                row_scatter(d, True).wait_send()

    else:

        @pl.when(giver)
        def _():
            @pl.loop(0, 8)
            def _(d):
                @pl.when(jnp.logical_not(home & (g == d)))
                def _():
                    row_scatter(d).wait_send()


class Moves:
    def __init__(self, first):
        self.first = first
        self.inputs, self.outputs = (0, 2) if first else (3, 2)

    def sends(self, r, index):
        early = (r < 2) & (index >= 2) if index < 4 else r >= 0
        return early if self.first else jnp.logical_not(early)

    def copies(self, ins, outs, sems, src, r, c, h, mate, other):
        (got, extra), (put_sem, got_sem, over_put, over_got) = outs, sems
        children = src if self.first else ins[0]

        def block(index, relay=False):
            place = got.at[h, pl.ds(index * NB, NB), :]
            if relay:
                return send(place, place, over_put.at[index], over_got.at[index], row=r, col=other)
            rows = pl.ds(pl.multiple_of((1 - r % 2) * 1536 + index * NB, NB), NB)
            return send(
                children.at[rows, :], place, put_sem.at[index], got_sem.at[index], row=mate, col=c
            )

        def aside():
            if self.first:
                rows = pl.ds(pl.multiple_of(r % 2 * 1536, NB), 1536)
                return send(
                    src.at[rows, :], extra, put_sem.at[6], got_sem.at[6], row=r, col=other
                )
            return send(
                ins[1].at[1 - r % 2], extra, put_sem.at[6], got_sem.at[6], row=mate, col=c
            )

        return block, aside


def share(members, source, extras, extra_shapes, collective_id):
    moves = Moves(members == 2)
    width = source.shape[1]
    dma = pltpu.SemaphoreType.DMA
    shape = jax.ShapeDtypeStruct
    row_shape = (2, 2, 8, 96, PIV) if members == 2 else (2, 1, PIV, width)
    out_shape = (
        shape((2, members, PIV, width), F32),
        shape(row_shape, F32),
        shape((members, 2, 8, 32, PIV), F32),
        *extra_shapes,
    )
    scratch = [
        *[pltpu.VMEM((PIV, PIV), F32)] * 3,
        dma((1,)),
        dma((3,)),
        dma((8,)),
        dma((members,)),
        dma((4,)),
        dma((4,)),
        dma((2,)),
        dma((2,)),
        dma((2, 16)),
        dma((members,)),
        dma((2, members)),
        dma((members, 4)),
        dma((members, 4)),
        dma((2,)),
        dma((16,)),
        dma((members,)),
        dma((8,)),
        dma((members,)),
        dma((8,)),
        dma((8,)),
        dma((2,)),
        dma((7,)),
        dma((7,)),
        dma((6,)),
        dma((6,)),
    ]

    def kernel(*refs):
        share_kernel(members, moves, *refs)

    cols, rows, inv, *extra = pl.pallas_call(
        kernel,
        out_shape=out_shape,
        in_specs=[pl.BlockSpec(memory_space=pl.ANY)] * (1 + len(extras)),
        out_specs=[pl.BlockSpec(memory_space=pl.ANY)] * len(out_shape),
        scratch_shapes=scratch,
        input_output_aliases={} if members == 2 else {3: 3},
        compiler_params=pltpu.CompilerParams(
            collective_id=collective_id, has_side_effects=True, vmem_limit_bytes=56 << 20
        ),
        cost_estimate=pl.CostEstimate(flops=10**10, bytes_accessed=1 << 25, transcendentals=0),
        name="share_panels_%d" % members,
    )(source, *extras)
    if members == 2:
        rows = rows.reshape(2, 1536, PIV)
    return cols, rows, inv.reshape(members, PIV, PIV), extra


def split(value):
    high = value.astype(jnp.bfloat16)
    return high, (value - high.astype(F32)).astype(jnp.bfloat16)


def left_terms(value):
    high, low = split(value)
    return jnp.concatenate([high, high, low], axis=1)


def right_terms(value):
    high, low = split(value)
    return jnp.concatenate([high, low, high], axis=0)


def dot(left, right):
    return jnp.dot(left, right, preferred_element_type=F32)


def column_block(panels, k, block):
    at = pl.multiple_of(block % 3 * NB, NB)
    return panels[block // 3, k, :, pl.ds(at, NB)]


def update_blocks(t, info, rowi, rowv, colj, colv, blocks):
    total = None
    for m in range(2):
        adds = []
        for u in range(4):
            first, second = blocks[m * 4 + u], blocks[8 + u]
            use = (rowv[m, t] > 0) & (colv[m, u] > 0)
            if m == 0:
                block = jnp.where(colj[m, u] // 3 == info[1], second[...], first[...])
            else:
                block = first[0]
            adds.append(jnp.where(use, block, 0.0))
        sum_m = jnp.concatenate(adds, axis=1)
        total = sum_m if total is None else total + sum_m
    return total


def block_specs():
    def own(u, place):
        def index(t, info, rowi, rowv, colj, colv):
            here = colj[0, u] // 3 == info[1]
            want = here if place == 0 else jnp.logical_not(here)
            row = rowi[0, t] + (info[0] * 6 if place == 0 else 0)
            return (jnp.where(want, row, 0), jnp.where(want, colj[0, u] % 3, 0))

        return pl.BlockSpec((NB, NB), index)

    def mates(u):
        def index(t, info, rowi, rowv, colj, colv):
            return (colj[1, u] // 3, rowi[1, t], colj[1, u] % 3)

        return pl.BlockSpec((1, NB, NB), index)

    return [
        *[own(u, 1) for u in range(4)],
        *[mates(u) for u in range(4)],
        *[own(u, 0) for u in range(4)],
    ]


def row_terms(value):
    high, low = split(value)
    return jnp.concatenate([high, low, high], axis=1)


def dot_t(left, right):
    return lax.dot_general(left, right, (((1,), (1,)), ((), ())), preferred_element_type=F32)


def panel_kernel(info, rowi, rowv, colj, colv, parent, rows, cols, inv, inv_part, *rest):
    blocks, (front, solved_cols, factors), (inv_terms,) = rest[:12], rest[12:15], rest[15:]
    t = pl.program_id(0)

    @pl.when(t == 0)
    def _():
        for k in range(2):
            inv_terms[k] = left_terms(inv[k])
        for m in range(2):
            k = info[0] if m == 0 else 1 - info[0]
            for u in range(4):
                block = right_terms(column_block(cols, k, colj[m, u]))
                solved = dot(inv_terms[k], block)
                solved = jnp.where(colv[m, u] > 0, solved, 0.0)
                solved_cols[m, :, u * NB : (u + 1) * NB] = right_terms(solved)
        for k in range(2):
            factors[k] = dot_t(left_terms(inv_part[k]), row_terms(rows[k]))

    total = parent[...] + update_blocks(t, info, rowi, rowv, colj, colv, blocks)
    for m in range(2):
        k = info[0] if m == 0 else 1 - info[0]
        block = rows[k, pl.ds(pl.multiple_of(rowi[m, t] * NB, NB), NB), :]
        solved = dot_t(left_terms(block), row_terms(inv[k]))
        solved = jnp.where(rowv[m, t] > 0, solved, 0.0)
        total = total - dot(left_terms(solved), solved_cols[m])
    front[...] = total


def panel_front(maps, parent, rows, cols, inv, inv_part, pieces):
    whole = pl.BlockSpec(memory_space=pltpu.VMEM)
    full = lambda shape: pl.BlockSpec(shape, lambda t, *_: (0,) * len(shape))
    grid_spec = pltpu.PrefetchScalarGridSpec(
        num_scalar_prefetch=5,
        grid=(2,),
        in_specs=[
            pl.BlockSpec((NB, 1024), lambda t, *_: (t, 0)),
            whole,
            whole,
            whole,
            whole,
            *block_specs(),
        ],
        out_specs=[
            pl.BlockSpec((NB, 1024), lambda t, *_: (t, 0)),
            full((2, 3 * PIV, 1024)),
            full((2, 32, 1536)),
        ],
        scratch_shapes=[pltpu.VMEM((2, PIV, 3 * PIV), jnp.bfloat16)],
    )
    return pl.pallas_call(
        panel_kernel,
        grid_spec=grid_spec,
        out_shape=(
            jax.ShapeDtypeStruct((PIV, 1024), F32),
            jax.ShapeDtypeStruct((2, 3 * PIV, 1024), jnp.bfloat16),
            jax.ShapeDtypeStruct((2, 32, 1536), F32),
        ),
        compiler_params=pltpu.CompilerParams(vmem_limit_bytes=60 << 20),
        cost_estimate=pl.CostEstimate(flops=10**10, bytes_accessed=1 << 25, transcendentals=0),
        name="panel_front",
    )(*maps, parent, rows, cols, inv, inv_part, *pieces)


def finish_kernel(info, rowi, rowv, colj, colv, parent, rows, inv, fcols, frows, finv, *rest):
    solved_cols, blocks, out = rest[0], rest[1:13], rest[13]
    inv_terms, par_cols, high, low, par_rows = rest[14:]
    t = pl.program_id(0)

    @pl.when(t == 0)
    def _():
        for m in range(2):
            k = info[0] if m == 0 else 1 - info[0]
            inv_terms[...] = row_terms(inv[k])
            for part in range(3):
                span = slice(part * PIV, (part + 1) * PIV)
                block = left_terms(rows[k, span, :])
                high[m, span, :], low[m, span, :] = split(dot_t(block, inv_terms[...]))
        inv_terms[...] = left_terms(finv[...])
        for u in range(4):
            span = slice(u * NB, (u + 1) * NB)
            par_cols[:, span] = right_terms(dot(inv_terms[...], right_terms(fcols[0, :, span])))
            for half in range(2):
                solved = dot(inv_terms[...], right_terms(frows[half, :, span])).T
                par_rows[half * 1024 + u * NB : half * 1024 + (u + 1) * NB, :] = solved

    solved = par_rows[pl.ds(pl.multiple_of(t * NB, NB), NB), :]
    total = parent[...] + update_blocks(t, info, rowi, rowv, colj, colv, blocks)
    out[...] = total - dot(left_terms(solved), par_cols[...])
    for m in range(2):

        @pl.when(rowv[m, t] > 0)
        def _():
            span = pl.ds(pl.multiple_of(rowi[m, t] * NB, NB), NB)
            left = jnp.concatenate([high[m, span, :], high[m, span, :], low[m, span, :]], axis=1)
            out[...] -= dot(left, solved_cols[m])

    @pl.when((info[2] == 0) & (t < 2))
    def _():
        out[...] = jnp.zeros_like(out)

    @pl.when(info[3] == 0)
    def _():
        row_ids = t * NB + lax.broadcasted_iota(jnp.int32, solved.shape, 0)
        col_ids = lax.broadcasted_iota(jnp.int32, solved.shape, 1)
        above = (info[2] == 0) & (col_ids > row_ids)
        out[:, :PIV] = jnp.where(above, 0.0, solved)


def finish(maps, parent, rows, inv, front_cols, front_rows, front_inv, solved_cols, pieces):
    whole = pl.BlockSpec(memory_space=pltpu.VMEM)
    grid_spec = pltpu.PrefetchScalarGridSpec(
        num_scalar_prefetch=5,
        grid=(8,),
        in_specs=[
            pl.BlockSpec((NB, 1024), lambda t, *_: (t, 0)),
            whole,
            whole,
            pl.BlockSpec((1, PIV, 1024), lambda t, info, *_: (info[1], 0, 0)),
            whole,
            whole,
            whole,
            *block_specs(),
        ],
        out_specs=pl.BlockSpec((NB, 1024), lambda t, *_: (t, 0)),
        scratch_shapes=[
            pltpu.VMEM((PIV, 3 * PIV), jnp.bfloat16),
            pltpu.VMEM((3 * PIV, 1024), jnp.bfloat16),
            pltpu.VMEM((2, 1536, PIV), jnp.bfloat16),
            pltpu.VMEM((2, 1536, PIV), jnp.bfloat16),
            pltpu.VMEM((2048, PIV), F32),
        ],
    )
    return pl.pallas_call(
        finish_kernel,
        grid_spec=grid_spec,
        out_shape=jax.ShapeDtypeStruct((2048, 1024), F32),
        compiler_params=pltpu.CompilerParams(vmem_limit_bytes=60 << 20),
        cost_estimate=pl.CostEstimate(flops=10**10, bytes_accessed=1 << 25, transcendentals=0),
        name="finish",
    )(*maps, parent, rows, inv, front_cols, front_rows, front_inv, solved_cols, *pieces)


def inverse_map(targets, first, places):
    blocks = first + jnp.arange(6, dtype=jnp.int32)
    usable = blocks >= PIV // NB
    wanted = jnp.clip(blocks - PIV // NB, 0, targets.shape[0] - 1)
    known = jnp.arange(targets.shape[0], dtype=jnp.int32)
    target = jnp.sum(jnp.where(known[None, :] == wanted[:, None], targets[None, :], 0), axis=1)
    hit = usable[:, None] & (target[:, None] == places[None, :])
    index = jnp.sum(jnp.where(hit, jnp.arange(6, dtype=jnp.int32)[:, None], 0), axis=0)
    return index.astype(jnp.int32), jnp.any(hit, axis=0).astype(jnp.int32)


def local(children, parent, relay_map):
    r = lax.axis_index("row")
    c = lax.axis_index("col")
    parity = r % 2
    g, h = c // 2, c % 2

    row_places = r * 8 + jnp.arange(8, dtype=jnp.int32)
    col_places = c * 4 + jnp.arange(4, dtype=jnp.int32)
    own_map = jnp.where(parity == 0, relay_map[0], relay_map[1])
    other_map = jnp.where(parity == 0, relay_map[1], relay_map[0])
    own_r = inverse_map(own_map, r * 6, row_places)
    other_r = inverse_map(other_map, r * 6, row_places)
    own_c = inverse_map(own_map, g * 6, col_places)
    other_c = inverse_map(other_map, g * 6, col_places)
    rowi, rowv = (jnp.stack(pair) for pair in zip(own_r, other_r))
    colj, colv = (jnp.stack(pair) for pair in zip(own_c, other_c))
    info = jnp.stack([parity, h, r, c]).astype(jnp.int32)
    maps = (info, rowi, rowv, colj, colv)

    shape = jax.ShapeDtypeStruct
    cols, rows, inv, (got, kept) = share(
        2, children, (), (shape((2, 1536, 768), F32), shape((1536, 768), F32)), 0
    )
    inv_part = lax.dynamic_slice_in_dim(inv, c * 32, 32, 1)
    pieces = lambda got: [kept] * 4 + [got] * 4 + [children] * 4
    front, solved_cols, factors = panel_front(
        maps, parent, rows, cols, inv, inv_part, pieces(got)
    )
    front_cols, front_rows, front_inv, (got, mates) = share(
        1,
        front,
        (children, factors, got),
        (shape((2, 1536, 768), F32), shape((32, 1536), F32)),
        1,
    )
    parent_out = finish(
        maps,
        parent,
        rows,
        inv,
        front_cols[:, 0],
        front_rows[:, 0],
        front_inv[0],
        solved_cols,
        pieces(got),
    )
    mine = lax.dynamic_index_in_dim(factors, parity, 0, keepdims=False)
    first = jnp.where(parity == 0, mine, mates)
    second = jnp.where(parity == 0, mates, mine)
    child_factor = jnp.concatenate([first, second], axis=1).T
    row_ids = r // 2 * 3072 + jnp.arange(3072, dtype=jnp.int32)
    col_ids = c * 32 + jnp.arange(32, dtype=jnp.int32)
    child_factor = jnp.where(row_ids[:, None] >= col_ids[None, :], child_factor, 0.0)
    return parent_out, child_factor


def solution(mesh):
    return jax.shard_map(
        local,
        mesh=mesh,
        in_specs=(P("row", "col"), P("row", "col"), P()),
        out_specs=(P("row", "col"), P("row", "col")),
        check_vma=False,
    )
```
